32 devices in a mesh: img: 8 (over z, x), sp: 4 (over y, core).
Axes of the slice: x: 2, y: 2, z: 4, core: 2. Of those that a mesh axis runs over, the one named last changes fastest.
Arguments:
- student: bfloat16 [96, 8, 8, 1280], P('img', 'sp')
- dino_feats: bfloat16 [48, 4, 4, 1536], P('img', 'sp'), may hold values from -6 to 6
- sam_feats: bfloat16 [48, 16, 16, 1280], P('img', 'sp'), may hold values from -6 to 6
- dino_proj: bfloat16 [1280, 1536], P('sp'), may hold values from -0.15625 to 0.15625
- sam_proj: bfloat16 [1280, 1280], P('sp'), may hold values from -0.15625 to 0.15625
- dino_list: int32 [48], replicated, may hold values from 0 to 95, as said below
- sam_list: int32 [48], replicated, may hold values from 0 to 95, as said below
- dino_row_weight: float32 [8, 3], replicated, may hold values from 0.2 to 1
- dino_col_weight: float32 [8, 4], replicated, may hold values from 0.1 to 0.6
- sam_start: int32 [8], replicated, may hold values from -2 to 14, as said below
- sam_row_weight: float32 [8, 4], replicated, may hold values from 0.2 to 1
- sam_col_weight: float32 [8, 16], replicated, may hold values from 0.05 to 0.35
Outputs:
- student_grad: bfloat16 [96, 8, 8, 1280], P('img', 'sp')
The draws below stay inside these ranges and needn't reach their ends.
Inputs may be any that keep to these rules, and one draw needn't show every extreme that they name: `dino_list`: entries are distinct student images; image i belongs to img index i // 12, and slot q lies on img index q // 6. One img index holds at most 2 slots of images of any one owner. Each owner has at most 12 images in the list, and some owner has exactly that many. `sam_list`: as for dino_list, drawn independently. sam_start[y] is 2 y - 2 + (y mod 2) or one more.
All inputs are finite; a program needn't handle non-finite values.
Results may differ from the reference program's by a relative error of at most 0.015.
Values may be sent and summed in bfloat16 or wider, within the bound.
No kernel may reach another device: no remote copies, remote signals or barrier semaphores. Data moves between devices by JAX's collectives and lax.ppermute only.
A program may use at most 64 MiB of HBM per device.

```python
import math
import jax
import jax.numpy as jnp
from jax import lax

D = 1280
DT = 1536
MT = 1280
IMG_DEV = 12
TEACH_DEV = 6
SC = 8
IMAGES = 96
SLOTS = 48
SR = 8
DR = 4
MR = 16
DC = 4
MC = 16
N_IMG = 8


def route_list(key):
    peer_count = N_IMG
    per_device = TEACH_DEV
    key_pair, key_shift, key_order, key_local = jax.random.split(key, 4)
    half_count = peer_count // 2
    pairing = jax.random.permutation(key_pair, peer_count)
    shift_by = jax.random.randint(key_shift, (half_count,), 0, per_device + 1)
    shift_by = shift_by.at[0].set(per_device)
    owner_loads = jnp.zeros((peer_count,), jnp.int32)
    owner_loads = owner_loads.at[pairing[:half_count]].set(per_device + shift_by)
    owner_loads = owner_loads.at[pairing[half_count:2 * half_count]].set(per_device - shift_by)
    owner_order = jax.random.permutation(key_order, peer_count)
    ordered_loads = owner_loads[owner_order]
    run_ends = jnp.cumsum(ordered_loads)
    run_starts = run_ends - ordered_loads
    positions = jnp.arange(peer_count * per_device, dtype=jnp.int32)
    run_index = jnp.sum((positions[:, None] >= run_ends[None, :]).astype(jnp.int32), axis=1)
    owner_of = owner_order[run_index]
    offset_in = positions - run_starts[run_index]
    local_keys = jax.random.split(key_local, peer_count)
    shuffles = jax.vmap(lambda sub_key: jax.random.permutation(sub_key, IMG_DEV))(local_keys)
    images = owner_of * IMG_DEV + shuffles[owner_of, offset_in]
    slot_index = jnp.arange(peer_count * per_device, dtype=jnp.int32)
    return images[slot_index % per_device * peer_count + slot_index // per_device].astype(jnp.int32)


def draw_dino_list(key, part):
    return route_list(jax.random.fold_in(key, 11))


def draw_sam_list(key, part):
    return route_list(jax.random.fold_in(key, 23))


def draw_sam_start(key, part):
    rows_index = jnp.arange(SR, dtype=jnp.int32)
    extra = jax.random.randint(jax.random.fold_in(key, 37), (SR,), 0, 2)
    extra = extra.at[0].set(0).at[SR - 1].set(1)
    return (2 * rows_index - 2 + rows_index % 2 + extra).astype(jnp.int32)


def draw_student(key, part):
    key_base, key_scale = jax.random.split(jax.random.fold_in(key, 51), 2)
    shape = (IMAGES, SR, SC, D)
    scales = 0.3 * jnp.exp(jax.random.uniform(key_scale, (IMAGES, SR, SC, 1), jnp.float32, 0.0, math.log(10.0)))
    base = jax.random.normal(key_base, shape, jnp.float32)
    return (base * scales).astype(jnp.bfloat16)


def block_levels(own_key, extent, pieces, smallest, high):
    level, own = 1.0, jax.random.fold_in(own_key, 6)
    for dim, blocks in pieces:
        draws = jnp.exp(jax.random.uniform(jax.random.fold_in(own, dim), (blocks,), jnp.float32, smallest / len(pieces), high / len(pieces)))
        level = level * jnp.repeat(draws, extent[dim] // blocks).reshape([-1 if axis == dim else 1 for axis in range(len(extent))])
    return level


def centred(rng, dims, scale, limit, cuts=(), kind=jnp.bfloat16):
    loudness = block_levels(rng, dims, cuts, -0.22, 0.18) if cuts else 1.0
    drawn = jax.random.normal(rng, dims, jnp.float32) * scale * loudness
    return jnp.minimum(jnp.maximum(drawn, -limit), limit).astype(kind)


def setup_inputs(seed: int = 0) -> dict:
    key_of = jax.random.split(jax.random.key(seed), 13)
    student = draw_student(jax.random.fold_in(key_of[12], 71), 0)
    dino_feats = centred(key_of[1], (SLOTS, DR, DC, DT), 1.0, 6.0, ((0, 8), (1, 4)))
    sam_feats = centred(key_of[2], (SLOTS, MR, MC, MT), 1.0, 6.0, ((0, 8), (1, 4)))
    dino_proj = centred(key_of[3], (D, DT), D ** -0.5, 0.15625, ((0, 4),))
    sam_proj = centred(key_of[4], (D, MT), D ** -0.5, 0.15625, ((0, 4),))
    dino_list = draw_dino_list(jax.random.fold_in(key_of[12], 71), 0)
    sam_list = draw_sam_list(jax.random.fold_in(key_of[12], 71), 0)
    dino_row_weight = jnp.clip(jax.random.uniform(key_of[7], (SR, 3), jnp.float32, 0.2, 1.0), 0.2, 1.0)
    dino_col_weight = jnp.clip(jax.random.uniform(key_of[8], (SC, DC), jnp.float32, 0.1, 0.6), 0.1, 0.6)
    sam_start = draw_sam_start(jax.random.fold_in(key_of[12], 71), 0)
    sam_row_weight = jnp.clip(jax.random.uniform(key_of[10], (SR, 4), jnp.float32, 0.2, 1.0), 0.2, 1.0)
    sam_col_weight = jnp.clip(jax.random.uniform(key_of[11], (SC, MC), jnp.float32, 0.05, 0.35), 0.05, 0.35)
    return {"student": student, "dino_feats": dino_feats, "sam_feats": sam_feats, "dino_proj": dino_proj, "sam_proj": sam_proj, "dino_list": dino_list, "sam_list": sam_list, "dino_row_weight": dino_row_weight, "dino_col_weight": dino_col_weight, "sam_start": sam_start, "sam_row_weight": sam_row_weight, "sam_col_weight": sam_col_weight}


HIGHEST = lax.Precision.HIGHEST
EPSILON = 1e-06

def tap_matrix(first_row, row_weight, padded_rows):
    columns = jnp.arange(padded_rows, dtype=jnp.int32)[None, :]
    matrix = jnp.zeros((row_weight.shape[0], padded_rows), jnp.float32)
    for tap_index in range(row_weight.shape[1]):
        hit = columns == (first_row + tap_index)[:, None]
        matrix = matrix + jnp.where(hit, row_weight[:, tap_index:tap_index + 1], 0.0)
    return matrix

def resample(matrix, col_weight, padded):
    down_rows = jnp.einsum('yk,kjc->yjc', matrix, padded.astype(jnp.float32), precision=HIGHEST)
    result = jnp.einsum('xj,yjc->yxc', col_weight, down_rows, precision=HIGHEST)
    return result.astype(jnp.bfloat16)

def cosine_back(student_rows, target, weight, mask_rows):
    predicted = jnp.dot(student_rows, weight, preferred_element_type=jnp.float32)
    target_wide = target.astype(jnp.float32)
    pred_norm = jnp.sqrt(lax.optimization_barrier(jnp.sum(predicted * predicted, axis=-1, keepdims=True)) + EPSILON)
    goal_norm = jnp.sqrt(lax.optimization_barrier(jnp.sum(target_wide * target_wide, axis=-1, keepdims=True)) + EPSILON)
    cosine = lax.optimization_barrier(jnp.sum(predicted * target_wide, axis=-1, keepdims=True)) / (pred_norm * goal_norm)
    feature_count = predicted.shape[-1]
    delta = feature_count * (cosine * predicted / (pred_norm * pred_norm) - target_wide / (pred_norm * goal_norm))
    delta = (delta * mask_rows).astype(jnp.bfloat16)
    grad_rows = lax.dot_general(delta, weight, (((1,), (1,)), ((), ())), preferred_element_type=jnp.float32)
    return grad_rows.astype(jnp.bfloat16)

def smooth_back(student_rows, target, weight, mask_rows):
    predicted = jnp.dot(student_rows, weight, preferred_element_type=jnp.float32)
    delta = jnp.clip(predicted - target.astype(jnp.float32), -1.0, 1.0)
    delta = (delta * mask_rows).astype(jnp.bfloat16)
    grad_rows = lax.dot_general(delta, weight, (((1,), (1,)), ((), ())), preferred_element_type=jnp.float32)
    return grad_rows.astype(jnp.bfloat16)

def reference(student, dino_feats, sam_feats, dino_proj, sam_proj, dino_list, sam_list, dino_row_weight, dino_col_weight, sam_start, sam_row_weight, sam_col_weight):
    grid_rows = student.shape[1]
    width = student.shape[-1]
    lines = jnp.arange(grid_rows, dtype=jnp.int32)
    dino_matrix = tap_matrix(lines // 2, dino_row_weight, dino_feats.shape[1] + 2)
    sam_matrix = tap_matrix(sam_start + 2, sam_row_weight, sam_feats.shape[1] + 4)

    def dino_one(slot_pair):
        features, image = slot_pair
        padded = jnp.pad(features, ((1, 1), (0, 0), (0, 0)))
        target = resample(dino_matrix, dino_col_weight, padded)
        student_rows = lax.dynamic_index_in_dim(student, image, 0, keepdims=False).reshape(-1, width)
        grad_rows = cosine_back(student_rows, target.reshape(student_rows.shape[0], -1), dino_proj, 1.0)
        return grad_rows.reshape(student.shape[1:])

    def sam_one(slot_pair):
        features, image = slot_pair
        padded = jnp.pad(features, ((2, 2), (0, 0), (0, 0)))
        target = resample(sam_matrix, sam_col_weight, padded)
        student_rows = lax.dynamic_index_in_dim(student, image, 0, keepdims=False).reshape(-1, width)
        grad_rows = smooth_back(student_rows, target.reshape(student_rows.shape[0], -1), sam_proj, 1.0)
        return grad_rows.reshape(student.shape[1:])
    dino_part = lax.map(dino_one, (dino_feats, dino_list))
    sam_part = lax.map(sam_one, (sam_feats, sam_list))
    total = jnp.zeros(student.shape, jnp.float32)
    total = total.at[dino_list].add(dino_part.astype(jnp.float32))
    total = total.at[sam_list].add(sam_part.astype(jnp.float32))
    return total.astype(jnp.bfloat16)
```

```python
import functools

import jax
import jax.numpy as jnp
from jax import lax
from jax.experimental import pallas as pl
from jax.experimental.pallas import tpu as pltpu
from jax.sharding import PartitionSpec as P

EPSILON = 1e-06
BF16 = jnp.bfloat16
F32 = jnp.float32
SMEM = pl.BlockSpec(memory_space=pltpu.SMEM)
VMEM = pl.BlockSpec(memory_space=pltpu.VMEM)
ANY = pl.BlockSpec(memory_space=pl.ANY)
VMEM_BYTES = 48 * 1024 * 1024


def params():
    return pltpu.CompilerParams(vmem_limit_bytes=VMEM_BYTES)


def split_dot(matrix, values):
    rows = matrix.shape[0]
    high = matrix.astype(BF16)
    low = (matrix - high.astype(F32)).astype(BF16)
    both = jnp.concatenate([high, low], axis=0)
    product = jnp.dot(both, values, preferred_element_type=F32)
    return product[:rows] + product[rows:]


def own_rows(list_ref, first, per_device, image_dev, capacity):
    owners = [lax.div(list_ref[first + i], image_dev) for i in range(per_device)]
    rows = []
    for i in range(per_device):
        position = jnp.int32(0)
        for j in range(i):
            position = position + jnp.where(owners[j] == owners[i], 1, 0)
        rows.append(owners[i] * capacity + position)
    return rows


def arrived_rows(list_ref, rank, slots, per_device, image_dev, capacity, row_of):
    for k in range(image_dev):
        row_of[k] = -1

    def source(peer, _):
        def slot(i, seen):
            image = list_ref[peer * per_device + i]
            mine = lax.div(image, image_dev) == rank

            @pl.when(mine)
            def _():
                row_of[image - rank * image_dev] = peer * capacity + seen

            return seen + jnp.where(mine, 1, 0)

        lax.fori_loop(0, per_device, slot, jnp.int32(0), unroll=True)
        return 0

    lax.fori_loop(0, slots // per_device, source, 0)


def pre_kernel(
    dims,
    dino_list,
    sam_list,
    start,
    row_weight,
    col_weight,
    dino_feats,
    sam_feats,
    dino_pack,
    own,
    core_part,
    edge_part,
):
    per_device, image_dev, capacity, grid_rows = dims
    rank = lax.axis_index("img")
    sp = lax.axis_index("sp")
    dino_pack[...] = jnp.zeros_like(dino_pack)
    for i, row in enumerate(own_rows(dino_list, rank * per_device, per_device, image_dev, capacity)):
        dino_pack[row] = dino_feats[i]

    even = lax.rem(sp, 2) == 0
    up, down = 2 * sp - 1, 2 * sp + 2
    targets = [2 * sp, 2 * sp + 1, jnp.where(even, down, up), jnp.where(even, up, down)]
    col_count = col_weight.shape[1]
    across = jnp.concatenate([col_weight[...]] * 4, axis=1)
    column_row = lax.broadcasted_iota(jnp.int32, across.shape, 1) // col_count
    blocks = []
    for y in targets:
        inside = jnp.logical_and(y >= 0, y < grid_rows)
        line = jnp.clip(y, 0, grid_rows - 1)
        first = start[line] - 4 * sp
        taps = jnp.zeros(across.shape, F32)
        for tap in range(row_weight.shape[1]):
            weight = jnp.where(inside, row_weight[line, tap], 0.0)
            taps = taps + jnp.where(column_row == first + tap, weight, 0.0)
        blocks.append(across * taps)
    matrix = jnp.concatenate(blocks, axis=0)
    wide = own.shape[1]
    half = wide // 2
    for i in range(per_device):
        result = split_dot(matrix, sam_feats[i])
        own[i] = result[:wide]
        core_part[i] = result[wide : wide + half].astype(BF16)
        edge_part[i] = result[wide + half :].astype(BF16)


def pack_kernel(dims, sam_list, own, core_part, edge_part, packed):
    per_device, image_dev, capacity = dims
    rank = lax.axis_index("img")
    even = lax.rem(lax.axis_index("sp"), 2) == 0
    half = core_part.shape[1]
    rows = own_rows(sam_list, rank * per_device, per_device, image_dev, capacity)
    for i, row in enumerate(rows):
        core = core_part[i].astype(F32)
        edge = edge_part[i].astype(F32)
        top = own[i, :half] + jnp.where(even, edge, core)
        bottom = own[i, half:] + jnp.where(even, core, edge)
        packed[row] = jnp.concatenate([top, bottom], axis=0).astype(BF16)


def target_kernel(
    dims, dino_list, row_weight, col_weight, here, core_side, edge_side, target, stacked, row_of
):
    slots, per_device, image_dev, capacity = dims
    rank = lax.axis_index("img")
    sp = lax.axis_index("sp")
    even = lax.rem(sp, 2) == 0
    arrived_rows(dino_list, rank, slots, per_device, image_dev, capacity, row_of)
    buffer_rows, cols = here.shape[0], here.shape[1]
    for b in range(buffer_rows):
        core = core_side[b].astype(F32)
        edge = edge_side[b].astype(F32)
        above = jnp.where(even, edge, core)
        below = jnp.where(even, core, edge)
        for k, values in enumerate((above, here[b].astype(F32), below)):
            at = (k * buffer_rows + b) * cols
            stacked[at : at + cols, :] = values
    values = stacked[...].astype(BF16)
    patch_cols = col_weight.shape[0]
    shape = (patch_cols, 3 * buffer_rows * cols)
    column = lax.broadcasted_iota(jnp.int32, shape, 1)
    tap_of = column // (buffer_rows * cols)
    row_at = (column // cols) % buffer_rows
    j_of = column % cols
    across = jnp.zeros(shape, F32)
    for j in range(cols):
        across = across + jnp.where(j_of == j, col_weight[:, j : j + 1], 0.0)
    lines = []
    for y in range(2):
        taps = jnp.zeros(shape, F32)
        for k in range(3):
            taps = taps + jnp.where(tap_of == k, row_weight[2 * sp + y, k], 0.0)
        lines.append(across * taps)
    base = jnp.concatenate(lines, axis=0)
    row_at = jnp.concatenate([row_at] * 2, axis=0)
    matrix = jnp.concatenate(
        [jnp.where(row_at == row_of[k], base, 0.0) for k in range(image_dev)], axis=0
    )
    target[...] = split_dot(matrix, values).astype(BF16)


def load_pieces(pieces, offsets, whole, sems):
    copies = []
    for n, (piece, offset) in enumerate(zip(pieces, offsets)):
        rows = piece.shape[0]
        place = pl.ds(pl.multiple_of(offset, 16), rows)
        copies.append(pltpu.make_async_copy(piece, whole.at[place, :], sems.at[n]))
    for copy in copies:
        copy.start()
    for copy in copies:
        copy.wait()


def piece_offsets(count, rows):
    if count == 1:
        return [0]
    sp = lax.axis_index("sp")
    half = jnp.where(sp >= 2, 2, 0)
    core = lax.rem(sp, 2)
    order = (half + core, half + 1 - core, 2 - half + core, 2 - half + 1 - core)
    return [o * rows for o in order]


def row_sum(values):
    return jnp.sum(values, axis=-1, keepdims=True)


def dino_kernel(count, student, target, *rest):
    pieces, (grad, whole, predicted, delta, sems) = rest[:count], rest[count:]
    load_pieces(pieces, piece_offsets(count, pieces[0].shape[0]), whole, sems)
    predicted[...] = jnp.dot(student[...], whole[...], preferred_element_type=F32)
    p = predicted[...]
    t = target[...].astype(F32)
    pred_inv = 1.0 / jnp.sqrt(row_sum(p * p) + EPSILON)
    goal_inv = 1.0 / jnp.sqrt(row_sum(t * t) + EPSILON)
    cosine = row_sum(p * t) * pred_inv * goal_inv
    features = p.shape[-1]
    delta[...] = (
        (features * pred_inv) * ((cosine * pred_inv) * p - goal_inv * t)
    ).astype(BF16)
    grad[...] = lax.dot_general(
        delta[...], whole[...], (((1,), (1,)), ((), ())), preferred_element_type=F32
    ).astype(BF16)


def sam_kernel(count, dims, sam_list, student, arrived, dino_grad, *rest):
    slots, per_device, image_dev, capacity = dims
    pieces, (out, whole, delta, row_of, sems) = rest[:count], rest[count:]
    rank = lax.axis_index("img")
    arrived_rows(sam_list, rank, slots, per_device, image_dev, capacity, row_of)
    load_pieces(pieces, piece_offsets(count, pieces[0].shape[0]), whole, sems)
    predicted = jnp.dot(student[...], whole[...], preferred_element_type=F32)
    patch = arrived.shape[1]
    for k in range(image_dev):
        row = row_of[k]
        target = arrived[jnp.maximum(row, 0)].astype(F32)
        error = jnp.clip(predicted[k * patch : (k + 1) * patch] - target, -1.0, 1.0)
        delta[k * patch : (k + 1) * patch, :] = jnp.where(row >= 0, error, 0.0).astype(BF16)
    back = lax.dot_general(
        delta[...], whole[...], (((1,), (1,)), ((), ())), preferred_element_type=F32
    )
    total = back.astype(BF16).astype(F32) + dino_grad[...].astype(F32)
    out[...] = total.astype(BF16)


def pair_perms(count):
    core = [(i, i ^ 1) for i in range(count)]
    edge = []
    for i in range(1, count - 1, 2):
        edge += [(i, i + 1), (i + 1, i)]
    return core, edge


def shards(
    student,
    dino_feats,
    sam_feats,
    dino_proj,
    sam_proj,
    dino_list,
    sam_list,
    dino_row_weight,
    dino_col_weight,
    sam_start,
    sam_row_weight,
    sam_col_weight,
):
    peers = lax.axis_size("img")
    sp_count = lax.axis_size("sp")
    images, rows_dev, patch_cols, width = student.shape
    slots = dino_list.shape[0]
    per_device = slots // peers
    capacity = (2 * per_device + peers - 1) // peers
    buffer_rows = peers * capacity
    patch = rows_dev * patch_cols
    grid_rows = dino_row_weight.shape[0]
    dino_cols, dino_width = dino_feats.shape[2:]
    sam_rows, sam_cols, sam_width = sam_feats.shape[1:]
    core_perm, edge_perm = pair_perms(sp_count)

    def core_swap(values):
        return lax.ppermute(values, "sp", core_perm)

    def edge_swap(values):
        return lax.ppermute(values, "sp", edge_perm)

    half_shape = jax.ShapeDtypeStruct((per_device, patch_cols, sam_width), BF16)
    dino_pack, own, core_part, edge_part = pl.pallas_call(
        functools.partial(pre_kernel, (per_device, images, capacity, grid_rows)),
        out_shape=(
            jax.ShapeDtypeStruct((buffer_rows, dino_cols, dino_width), BF16),
            jax.ShapeDtypeStruct((per_device, patch, sam_width), F32),
            half_shape,
            half_shape,
        ),
        in_specs=[SMEM] * 4 + [VMEM] * 3,
        out_specs=(VMEM,) * 4,
        compiler_params=params(),
        name="pre",
    )(
        dino_list,
        sam_list,
        sam_start,
        sam_row_weight,
        sam_col_weight,
        dino_feats.reshape(per_device, dino_cols, dino_width),
        sam_feats.reshape(per_device, sam_rows * sam_cols, sam_width),
    )

    edge_got = edge_swap(edge_part)
    core_got = core_swap(core_part)
    dino_got = lax.all_to_all(dino_pack, "img", split_axis=0, concat_axis=0, tiled=True)

    sam_pack = pl.pallas_call(
        functools.partial(pack_kernel, (per_device, images, capacity)),
        out_shape=jax.ShapeDtypeStruct((buffer_rows, patch, sam_width), BF16),
        in_specs=[SMEM] + [VMEM] * 3,
        out_specs=VMEM,
        compiler_params=params(),
        name="pack",
    )(sam_list, own, core_got, edge_got)
    sam_got = lax.all_to_all(sam_pack, "img", split_axis=0, concat_axis=0, tiled=True)

    dino_core, dino_edge = core_swap(dino_got), edge_swap(dino_got)
    if sp_count == 4:
        chip_perm = [(i, i ^ 2) for i in range(4)]

        def gather(shard):
            across = lax.ppermute(shard, "sp", chip_perm)
            return [shard, core_swap(shard), across, core_swap(across)]

        dino_pieces, sam_pieces = gather(dino_proj), gather(sam_proj)
    else:
        dino_pieces = [lax.all_gather(dino_proj, "sp", axis=0, tiled=True)]
        sam_pieces = [lax.all_gather(sam_proj, "sp", axis=0, tiled=True)]

    target = pl.pallas_call(
        functools.partial(target_kernel, (slots, per_device, images, capacity)),
        out_shape=jax.ShapeDtypeStruct((images * patch, dino_width), BF16),
        in_specs=[SMEM, SMEM] + [VMEM] * 4,
        out_specs=VMEM,
        scratch_shapes=[
            pltpu.VMEM((3 * buffer_rows * dino_cols, dino_width), F32),
            pltpu.SMEM((images,), jnp.int32),
        ],
        compiler_params=params(),
        name="target",
    )(dino_list, dino_row_weight, dino_col_weight, dino_got, dino_core, dino_edge)

    rows = student.reshape(images * patch, width)
    count = len(dino_pieces)
    dino_grad = pl.pallas_call(
        functools.partial(dino_kernel, count),
        out_shape=jax.ShapeDtypeStruct(rows.shape, BF16),
        in_specs=[VMEM, VMEM] + [ANY] * count,
        out_specs=VMEM,
        scratch_shapes=[
            pltpu.VMEM((width, dino_width), BF16),
            pltpu.VMEM((rows.shape[0], dino_width), F32),
            pltpu.VMEM((rows.shape[0], dino_width), BF16),
            pltpu.SemaphoreType.DMA((count,)),
        ],
        compiler_params=params(),
        name="dino",
    )(rows, target, *dino_pieces)

    out = pl.pallas_call(
        functools.partial(sam_kernel, count, (slots, per_device, images, capacity)),
        out_shape=jax.ShapeDtypeStruct(rows.shape, BF16),
        in_specs=[SMEM] + [VMEM] * 3 + [ANY] * count,
        out_specs=VMEM,
        scratch_shapes=[
            pltpu.VMEM((width, sam_width), BF16),
            pltpu.VMEM((rows.shape[0], sam_width), BF16),
            pltpu.SMEM((images,), jnp.int32),
            pltpu.SemaphoreType.DMA((count,)),
        ],
        compiler_params=params(),
        name="sam",
    )(sam_list, rows, sam_got, dino_grad, *sam_pieces)
    return out.reshape(student.shape)


def solution(mesh):
    placed = (
        P("img", "sp", None, None),
        P("img", "sp", None, None),
        P("img", "sp", None, None),
        P("sp", None),
        P("sp", None),
        P(),
        P(),
        P(),
        P(),
        P(),
        P(),
        P(),
    )
    return jax.shard_map(
        shards, mesh=mesh, in_specs=placed, out_specs=P("img", "sp", None, None), check_vma=False
    )
```

```python
import functools

import jax
import jax.numpy as jnp
from jax import lax
from jax.experimental import pallas as pl
from jax.experimental.pallas import tpu as pltpu
from jax.sharding import PartitionSpec as P

EPSILON = 1e-06
BF16 = jnp.bfloat16
F32 = jnp.float32
SMEM = pl.BlockSpec(memory_space=pltpu.SMEM)
VMEM = pl.BlockSpec(memory_space=pltpu.VMEM)
ANY = pl.BlockSpec(memory_space=pl.ANY)
VMEM_BYTES = 24 * 1024 * 1024
ALL_BYTES = 60 * 1024 * 1024


def params(vmem_bytes=VMEM_BYTES):
    return pltpu.CompilerParams(vmem_limit_bytes=vmem_bytes)


def split_dot(matrix, values):
    rows = matrix.shape[0]
    high = matrix.astype(BF16)
    low = (matrix - high.astype(F32)).astype(BF16)
    both = jnp.concatenate([high, low], axis=0)
    product = jnp.dot(both, values, preferred_element_type=F32)
    return product[:rows] + product[rows:]


def own_rows(list_ref, rank, per_device, image_dev, capacity):
    first = rank * per_device
    owners = [lax.div(list_ref[first + i], image_dev) for i in range(per_device)]
    rows = []
    for i in range(per_device):
        position = jnp.int32(0)
        for j in range(i):
            position = position + jnp.where(owners[j] == owners[i], 1, 0)
        rows.append(owners[i] * capacity + position)
    return rows


def arrived_rows(list_ref, rank, slots, per_device, image_dev, capacity, row_of):
    for k in range(image_dev):
        row_of[k] = -1

    def source(peer, _):
        def slot(i, seen):
            image = list_ref[peer * per_device + i]
            mine = lax.div(image, image_dev) == rank

            @pl.when(mine)
            def _():
                row_of[image - rank * image_dev] = peer * capacity + seen

            return seen + jnp.where(mine, 1, 0)

        lax.fori_loop(0, per_device, slot, jnp.int32(0), unroll=True)
        return 0

    lax.fori_loop(0, slots // per_device, source, 0)


def pre_kernel(dims, start, row_weight, col_weight, sam_feats, own, core_part, edge_part):
    per_device, grid_rows = dims
    sp = lax.axis_index("sp")
    even = lax.rem(sp, 2) == 0
    up, down = 2 * sp - 1, 2 * sp + 2
    targets = [2 * sp, 2 * sp + 1, jnp.where(even, down, up), jnp.where(even, up, down)]
    col_count = col_weight.shape[1]
    across = jnp.concatenate([col_weight[...]] * 4, axis=1)
    column_row = lax.broadcasted_iota(jnp.int32, across.shape, 1) // col_count
    blocks = []
    for y in targets:
        inside = jnp.logical_and(y >= 0, y < grid_rows)
        line = jnp.clip(y, 0, grid_rows - 1)
        first_row = start[line] - 4 * sp
        taps = jnp.zeros(across.shape, F32)
        for tap in range(row_weight.shape[0]):
            weight = jnp.where(inside, row_weight[tap, line], 0.0)
            taps = taps + jnp.where(column_row == first_row + tap, weight, 0.0)
        blocks.append(across * taps)
    matrix = jnp.concatenate(blocks, axis=0)
    wide = own.shape[1]
    half = wide // 2
    for i in range(per_device):
        result = split_dot(matrix, sam_feats[i])
        own[i] = result[:wide]
        core_part[i] = result[wide : wide + half].astype(BF16)
        edge_part[i] = result[wide + half :].astype(BF16)


def pack_kernel(
    dims, dino_list, sam_list, dino_feats, own, core_part, edge_part, packed
):
    per_device, image_dev, capacity = dims
    rank = lax.axis_index("img")
    even = lax.rem(lax.axis_index("sp"), 2) == 0
    half, sam_width = core_part.shape[1:]
    patch = 2 * half
    sam_blocks = sam_width // 128
    for i, row in enumerate(own_rows(sam_list, rank, per_device, image_dev, capacity)):
        core = core_part[i].astype(F32)
        edge = edge_part[i].astype(F32)
        top = own[i, :half] + jnp.where(even, edge, core)
        bottom = own[i, half:] + jnp.where(even, core, edge)
        values = jnp.concatenate([top, bottom], axis=0).astype(BF16)
        for n in range(sam_blocks):
            packed[row, n * patch : (n + 1) * patch, :] = values[:, n * 128 : (n + 1) * 128]
    first = sam_blocks * patch
    packed[:, first:, :] = jnp.zeros((packed.shape[0], packed.shape[1] - first, 128), BF16)
    for i, row in enumerate(own_rows(dino_list, rank, per_device, image_dev, capacity)):
        values = dino_feats[i].astype(F32)
        blocks = [values[:, n * 128 : (n + 1) * 128] for n in range(values.shape[1] // 128)]
        packed[row, first:, :] = jnp.concatenate(blocks, axis=0).astype(BF16)


def select_kernel(dims, dino_list, arrived, chosen, row_of):
    slots, per_device, image_dev, capacity = dims
    rank = lax.axis_index("img")
    arrived_rows(dino_list, rank, slots, per_device, image_dev, capacity, row_of)
    first = arrived.shape[1] - chosen.shape[1]
    for k in range(image_dev):
        row = row_of[k]
        values = arrived[jnp.maximum(row, 0), first:, :]
        chosen[k] = jnp.where(row >= 0, values, jnp.zeros_like(values))


def target_kernel(row_weight, col_weight, here, core_side, edge_side, target, stacked):
    sp = lax.axis_index("sp")
    even = lax.rem(sp, 2) == 0
    images, blocks = here.shape[0], here.shape[1] // 8
    cols = col_weight.shape[1]
    core = core_side[...].astype(F32)
    edge = edge_side[...].astype(F32)
    above = jnp.where(even, edge, core)
    below = jnp.where(even, core, edge)
    for k, values in enumerate((above, here[...].astype(F32), below)):
        for n in range(blocks):
            part = values[:, 8 * n : 8 * n + 8, :].reshape(images * 8, 128)
            stacked[k * images * 8 : (k + 1) * images * 8, n * 128 : (n + 1) * 128] = part.astype(BF16)
    patch_cols = col_weight.shape[0]
    shape = (patch_cols, 3 * images * 8)
    column = lax.broadcasted_iota(jnp.int32, shape, 1)
    tap_of = column // (images * 8)
    image_of = (column // 8) % images
    block_of = (column // cols) % 2
    j_of = column % cols
    across = jnp.zeros(shape, F32)
    for j in range(cols):
        across = across + jnp.where(j_of == j, col_weight[:, j : j + 1], 0.0)
    lines = []
    for y in range(2):
        taps = jnp.zeros(shape, F32)
        for k in range(3):
            taps = taps + jnp.where(tap_of == k, row_weight[k, 2 * sp + y], 0.0)
        lines.append(across * taps)
    base = jnp.concatenate(lines, axis=0)
    image_of = jnp.concatenate([image_of] * 2, axis=0)
    block_of = jnp.concatenate([block_of] * 2, axis=0)
    matrix = jnp.concatenate(
        [
            jnp.where(jnp.logical_and(image_of == k, block_of == side), base, 0.0)
            for side in range(2)
            for k in range(images)
        ],
        axis=0,
    )
    result = split_dot(matrix, stacked[...]).astype(BF16)
    rows = target.shape[0]
    for n in range(blocks):
        for side in range(2):
            at = (2 * n + side) * 128
            target[:, at : at + 128] = result[side * rows : (side + 1) * rows, n * 128 : (n + 1) * 128]


def load_whole(pieces, by_neighbour, whole, sems, first_sem):
    rows = pieces[0].shape[0]
    places = [(pieces[0], 0)]
    if len(pieces) > 1:
        sp = lax.axis_index("sp")
        here, core = sp // 2 * 2, lax.rem(sp, 2)
        first = lax.rem(lax.axis_index("img"), 2) * (rows // 2) if by_neighbour else 0
        places = [(pieces[0], (here + core) * rows), (pieces[1], (here + 1 - core) * rows)]
        for far, at in ((2 - here + core, 2), (3 - here - core, 4)):
            places.append((pieces[at], far * rows + first))
            places.append((pieces[at + 1], far * rows + rows // 2 - first))
    copies = []
    for n, (piece, offset) in enumerate(places):
        place = pl.ds(pl.multiple_of(offset, 16), piece.shape[0])
        copies.append(pltpu.make_async_copy(piece, whole.at[place, :], sems.at[first_sem + n]))
    for copy in copies:
        copy.start()
    return copies


def row_sum(values):
    return jnp.sum(values, axis=-1, keepdims=True)


def sam_kernel(
    counts, dims, sam_list, student, arrived, *rest
):
    slots, per_device, image_dev, capacity = dims
    sam_pieces, dino_pieces = rest[: counts[0]], rest[counts[0] : sum(counts)]
    grad, predicted, dino_whole, rows_in, packs_in, sam_whole, delta, row_of, sems = rest[sum(counts) :]
    rows_copy = pltpu.make_async_copy(student, rows_in, sems.at[0])
    packs_copy = pltpu.make_async_copy(arrived, packs_in, sems.at[1])
    rows_copy.start()
    sam_copies = load_whole(sam_pieces, True, sam_whole, sems, 2)
    packs_copy.start()
    dino_copies = load_whole(dino_pieces, False, dino_whole, sems, 2 + counts[0])
    rank = lax.axis_index("img")
    arrived_rows(sam_list, rank, slots, per_device, image_dev, capacity, row_of)
    for copy in (rows_copy, *sam_copies):
        copy.wait()
    sam_predicted = jnp.dot(rows_in[...], sam_whole[...], preferred_element_type=F32)
    packs_copy.wait()
    patch = rows_in.shape[0] // image_dev
    for k in range(image_dev):
        row = row_of[k]
        at = jnp.maximum(row, 0)
        rows = slice(k * patch, (k + 1) * patch)
        for n in range(sam_whole.shape[1] // 128):
            columns = slice(n * 128, (n + 1) * 128)
            target = packs_in[at, n * patch : (n + 1) * patch, :].astype(F32)
            error = jnp.clip(sam_predicted[rows, columns] - target, -1.0, 1.0)
            delta[rows, columns] = jnp.where(row >= 0, error, 0.0).astype(BF16)
    grad[...] = lax.dot_general(
        delta[...], sam_whole[...], (((1,), (1,)), ((), ())), preferred_element_type=F32
    ).astype(BF16)
    for copy in dino_copies:
        copy.wait()
    predicted[...] = jnp.dot(rows_in[...], dino_whole[...], preferred_element_type=F32)


def dino_kernel(predicted, target, sam_grad, whole, out, delta):
    p = predicted[...]
    t = target[...].astype(F32)
    pred_inv = 1.0 / jnp.sqrt(row_sum(p * p) + EPSILON)
    goal_inv = 1.0 / jnp.sqrt(row_sum(t * t) + EPSILON)
    cosine = row_sum(p * t) * pred_inv * goal_inv
    features = p.shape[-1]
    delta[...] = (
        (features * pred_inv) * ((cosine * pred_inv) * p - goal_inv * t)
    ).astype(BF16)
    back = lax.dot_general(
        delta[...], whole[...], (((1,), (1,)), ((), ())), preferred_element_type=F32
    )
    total = back.astype(BF16).astype(F32) + sam_grad[...].astype(F32)
    out[...] = total.astype(BF16)


def after(first, *rest):
    return lax.optimization_barrier((first, *rest))


def pair_perms(count):
    core = [(i, i ^ 1) for i in range(count)]
    edge = []
    for i in range(1, count - 1, 2):
        edge += [(i, i + 1), (i + 1, i)]
    return core, edge


def shards(
    student,
    dino_feats,
    sam_feats,
    dino_proj,
    sam_proj,
    dino_list,
    sam_list,
    dino_row_weight,
    dino_col_weight,
    sam_start,
    sam_row_weight,
    sam_col_weight,
):
    peers = lax.axis_size("img")
    sp_count = lax.axis_size("sp")
    images, rows_dev, patch_cols, width = student.shape
    slots = dino_list.shape[0]
    per_device = slots // peers
    capacity = (2 * per_device + peers - 1) // peers
    buffer_rows = peers * capacity
    patch = rows_dev * patch_cols
    grid_rows = dino_row_weight.shape[0]
    dino_cols, dino_width = dino_feats.shape[2:]
    sam_rows, sam_cols, sam_width = sam_feats.shape[1:]
    core_perm, edge_perm = pair_perms(sp_count)

    def core_swap(values):
        return lax.ppermute(values, "sp", core_perm)

    def edge_swap(values):
        return lax.ppermute(values, "sp", edge_perm)

    dims = (per_device, images, capacity)
    shared = sp_count == 4 and peers % 2 == 0
    pack_rows = patch * sam_width // 128 + dino_cols * dino_width // 128
    half_shape = jax.ShapeDtypeStruct((per_device, patch_cols, sam_width), BF16)
    own, core_part, edge_part = pl.pallas_call(
        functools.partial(pre_kernel, (per_device, grid_rows)),
        out_shape=(
            jax.ShapeDtypeStruct((per_device, patch, sam_width), F32),
            half_shape,
            half_shape,
        ),
        in_specs=[SMEM] * 2 + [VMEM] * 2,
        out_specs=(VMEM,) * 3,
        compiler_params=params(ALL_BYTES),
        name="pre",
    )(
        sam_start,
        sam_row_weight.T,
        sam_col_weight,
        sam_feats.reshape(per_device, sam_rows * sam_cols, sam_width),
    )
    edge_got = edge_swap(edge_part)
    core_got = core_swap(core_part)
    packed = pl.pallas_call(
        functools.partial(pack_kernel, dims),
        out_shape=jax.ShapeDtypeStruct((buffer_rows, pack_rows, 128), BF16),
        in_specs=[SMEM] * 2 + [VMEM] * 4,
        out_specs=VMEM,
        compiler_params=params(ALL_BYTES),
        name="pack",
    )(
        dino_list,
        sam_list,
        dino_feats.reshape(per_device, dino_cols, dino_width),
        own,
        core_got,
        edge_got,
    )

    arrived = lax.all_to_all(packed, "img", split_axis=0, concat_axis=0, tiled=True)

    if shared:
        chip_perm = [(i, i ^ 2) for i in range(4)]
        near_perm = [(i, i ^ 1) for i in range(peers)]
        half = sam_proj.shape[0] // 2
        near = lax.dynamic_slice_in_dim(sam_proj, lax.axis_index("img") % 2 * half, half, 0)
        _, _, near = after(edge_got, core_got, near)
        sam_far = [lax.ppermute(near, "sp", chip_perm)]
        sam_far[0], _, dino_shard = after(sam_far[0], packed, dino_proj)
        sam_far.append(lax.ppermute(sam_far[0], "img", near_perm))
        dino_far = [
            lax.ppermute(part, "sp", chip_perm) for part in (dino_shard[:half], dino_shard[half:])
        ]
        dino_pieces = [dino_proj, core_swap(dino_proj), *dino_far, *map(core_swap, dino_far)]
        sam_pieces = [sam_proj, core_swap(sam_proj), *sam_far, *map(core_swap, sam_far)]
    else:
        dino_pieces = [lax.all_gather(dino_proj, "sp", axis=0, tiled=True)]
        sam_pieces = [lax.all_gather(sam_proj, "sp", axis=0, tiled=True)]

    dino_rows = dino_cols * dino_width // 128
    chosen = pl.pallas_call(
        functools.partial(select_kernel, (slots, *dims)),
        out_shape=jax.ShapeDtypeStruct((images, dino_rows, 128), BF16),
        in_specs=[SMEM, VMEM],
        out_specs=VMEM,
        scratch_shapes=[pltpu.SMEM((images,), jnp.int32)],
        compiler_params=params(),
        name="select",
    )(dino_list, arrived)
    target = pl.pallas_call(
        target_kernel,
        out_shape=jax.ShapeDtypeStruct((images * patch, dino_width), BF16),
        in_specs=[SMEM] + [VMEM] * 4,
        out_specs=VMEM,
        scratch_shapes=[pltpu.VMEM((3 * images * 8, dino_width // 2), BF16)],
        compiler_params=params(),
        name="target",
    )(dino_row_weight.T, dino_col_weight, chosen, core_swap(chosen), edge_swap(chosen))

    rows = student.reshape(images * patch, width)
    counts = (len(sam_pieces), len(dino_pieces))
    sam_grad, dino_predicted, dino_whole = pl.pallas_call(
        functools.partial(sam_kernel, counts, (slots, *dims)),
        out_shape=(
            jax.ShapeDtypeStruct(rows.shape, BF16),
            jax.ShapeDtypeStruct((rows.shape[0], dino_width), F32),
            jax.ShapeDtypeStruct((width, dino_width), BF16),
        ),
        in_specs=[SMEM] + [ANY] * (2 + sum(counts)),
        out_specs=(VMEM,) * 3,
        scratch_shapes=[
            pltpu.VMEM(rows.shape, BF16),
            pltpu.VMEM(arrived.shape, BF16),
            pltpu.VMEM((width, sam_width), BF16),
            pltpu.VMEM((rows.shape[0], sam_width), BF16),
            pltpu.SMEM((images,), jnp.int32),
            pltpu.SemaphoreType.DMA((2 + sum(counts),)),
        ],
        compiler_params=params(),
        name="sam",
    )(sam_list, rows, arrived, *sam_pieces, *dino_pieces)
    out = pl.pallas_call(
        dino_kernel,
        out_shape=jax.ShapeDtypeStruct(rows.shape, BF16),
        in_specs=[VMEM] * 4,
        out_specs=VMEM,
        scratch_shapes=[pltpu.VMEM((rows.shape[0], dino_width), BF16)],
        compiler_params=params(),
        name="dino",
    )(dino_predicted, target, sam_grad, dino_whole)
    return out.reshape(student.shape)


def solution(mesh):
    placed = (
        P("img", "sp", None, None),
        P("img", "sp", None, None),
        P("img", "sp", None, None),
        P("sp", None),
        P("sp", None),
        P(),
        P(),
        P(),
        P(),
        P(),
        P(),
        P(),
    )
    return jax.shard_map(
        shards, mesh=mesh, in_specs=placed, out_specs=P("img", "sp", None, None), check_vma=False
    )
```

```python
import functools

import jax
import jax.numpy as jnp
from jax import lax
from jax.experimental import pallas as pl
from jax.experimental.pallas import tpu as pltpu
from jax.sharding import PartitionSpec as P

EPSILON = 1e-06
BF16 = jnp.bfloat16
F32 = jnp.float32
SMEM = pl.BlockSpec(memory_space=pltpu.SMEM)
VMEM = pl.BlockSpec(memory_space=pltpu.VMEM)
ANY = pl.BlockSpec(memory_space=pl.ANY)
VMEM_BYTES = 24 * 1024 * 1024
ALL_BYTES = 60 * 1024 * 1024


def params(vmem_bytes=VMEM_BYTES):
    return pltpu.CompilerParams(vmem_limit_bytes=vmem_bytes)


def split_dot(matrix, values):
    rows = matrix.shape[0]
    high = matrix.astype(BF16)
    low = (matrix - high.astype(F32)).astype(BF16)
    both = jnp.concatenate([high, low], axis=0)
    product = jnp.dot(both, values, preferred_element_type=F32)
    return product[:rows] + product[rows:]


def own_rows(list_ref, rank, per_device, image_dev, capacity):
    first = rank * per_device
    owners = [lax.div(list_ref[first + i], image_dev) for i in range(per_device)]
    rows = []
    for i in range(per_device):
        position = jnp.int32(0)
        for j in range(i):
            position = position + jnp.where(owners[j] == owners[i], 1, 0)
        rows.append(owners[i] * capacity + position)
    return rows


def arrived_rows(list_ref, rank, slots, per_device, image_dev, capacity, row_of):
    for k in range(image_dev):
        row_of[k] = -1

    def source(peer, _):
        def slot(i, seen):
            image = list_ref[peer * per_device + i]
            mine = lax.div(image, image_dev) == rank

            @pl.when(mine)
            def _():
                row_of[image - rank * image_dev] = peer * capacity + seen

            return seen + jnp.where(mine, 1, 0)

        lax.fori_loop(0, per_device, slot, jnp.int32(0), unroll=True)
        return 0

    lax.fori_loop(0, slots // per_device, source, 0)


def pre_kernel(dims, start, row_weight, col_weight, sam_feats, own, core_part, edge_part):
    per_device, grid_rows = dims
    sp = lax.axis_index("sp")
    even = lax.rem(sp, 2) == 0
    up, down = 2 * sp - 1, 2 * sp + 2
    targets = [2 * sp, 2 * sp + 1, jnp.where(even, down, up), jnp.where(even, up, down)]
    col_count = col_weight.shape[1]
    across = jnp.concatenate([col_weight[...]] * 4, axis=1)
    column_row = lax.broadcasted_iota(jnp.int32, across.shape, 1) // col_count
    blocks = []
    for y in targets:
        inside = jnp.logical_and(y >= 0, y < grid_rows)
        line = jnp.clip(y, 0, grid_rows - 1)
        first_row = start[line] - 4 * sp
        taps = jnp.zeros(across.shape, F32)
        for tap in range(row_weight.shape[0]):
            weight = jnp.where(inside, row_weight[tap, line], 0.0)
            taps = taps + jnp.where(column_row == first_row + tap, weight, 0.0)
        blocks.append(across * taps)
    matrix = jnp.concatenate(blocks, axis=0)
    wide = own.shape[1]
    half = wide // 2
    for i in range(per_device):
        result = split_dot(matrix, sam_feats[i])
        own[i] = result[:wide]
        core_part[i] = result[wide : wide + half].astype(BF16)
        edge_part[i] = result[wide + half :].astype(BF16)


def pack_kernel(
    dims, dino_list, sam_list, dino_feats, own, core_part, edge_part, packed
):
    per_device, image_dev, capacity = dims
    rank = lax.axis_index("img")
    even = lax.rem(lax.axis_index("sp"), 2) == 0
    half, sam_width = core_part.shape[1:]
    patch = 2 * half
    sam_blocks = sam_width // 128
    for i, row in enumerate(own_rows(sam_list, rank, per_device, image_dev, capacity)):
        core = core_part[i].astype(F32)
        edge = edge_part[i].astype(F32)
        top = own[i, :half] + jnp.where(even, edge, core)
        bottom = own[i, half:] + jnp.where(even, core, edge)
        values = jnp.concatenate([top, bottom], axis=0).astype(BF16)
        for n in range(sam_blocks):
            packed[row, n * patch : (n + 1) * patch, :] = values[:, n * 128 : (n + 1) * 128]
    first = sam_blocks * patch
    packed[:, first:, :] = jnp.zeros((packed.shape[0], packed.shape[1] - first, 128), BF16)
    for i, row in enumerate(own_rows(dino_list, rank, per_device, image_dev, capacity)):
        values = dino_feats[i].astype(F32)
        blocks = [values[:, n * 128 : (n + 1) * 128] for n in range(values.shape[1] // 128)]
        packed[row, first:, :] = jnp.concatenate(blocks, axis=0).astype(BF16)


def tables_kernel(
    image_dev, row_weight, col_weight, student, matrix
):
    sp = lax.axis_index("sp")
    patch_cols, cols = col_weight.shape
    shape = (patch_cols, 3 * image_dev * 2 * cols)
    column = lax.broadcasted_iota(jnp.int32, shape, 1)
    tap_of = column // (image_dev * 2 * cols)
    image_of = (column // (2 * cols)) % image_dev
    block_of = (column // cols) % 2
    j_of = column % cols
    across = jnp.zeros(shape, F32)
    for j in range(cols):
        across = across + jnp.where(j_of == j, col_weight[:, j : j + 1], 0.0)
    lines = []
    for y in range(2):
        taps = jnp.zeros(shape, F32)
        for k in range(3):
            taps = taps + jnp.where(tap_of == k, row_weight[k, 2 * sp + y], 0.0)
        lines.append(across * taps)
    base = jnp.concatenate(lines, axis=0)
    image_of = jnp.concatenate([image_of] * 2, axis=0)
    block_of = jnp.concatenate([block_of] * 2, axis=0)
    high = base.astype(BF16).astype(F32)
    patch = base.shape[0]
    for part, values in enumerate((high, base - high)):
        for side in range(2):
            for k in range(image_dev):
                at = ((part * 2 + side) * image_dev + k) * patch
                mine = jnp.logical_and(image_of == k, block_of == side)
                matrix[at : at + patch, :] = jnp.where(mine, values, 0.0).astype(BF16)


def select_kernel(dims, dino_list, arrived, chosen, rows_of):
    slots, per_device, image_dev, capacity = dims
    rank = lax.axis_index("img")
    arrived_rows(dino_list, rank, slots, per_device, image_dev, capacity, rows_of)
    first = arrived.shape[1] - chosen.shape[1]
    for k in range(chosen.shape[0]):
        row = rows_of[k]
        values = arrived[jnp.maximum(row, 0), first:, :]
        chosen[k] = jnp.where(row >= 0, values, jnp.zeros_like(values))


def load_whole(pieces, by_neighbour, whole, sems, first_sem):
    rows = pieces[0].shape[0]
    places = [(pieces[0], 0)]
    if len(pieces) > 1:
        sp = lax.axis_index("sp")
        here, core = sp // 2 * 2, lax.rem(sp, 2)
        first = lax.rem(lax.axis_index("img"), 2) * (rows // 2) if by_neighbour else 0
        places = [(pieces[0], (here + core) * rows), (pieces[1], (here + 1 - core) * rows)]
        for far, at in ((2 - here + core, 2), (3 - here - core, 4)):
            places.append((pieces[at], far * rows + first))
            places.append((pieces[at + 1], far * rows + rows // 2 - first))
    copies = []
    for n, (piece, offset) in enumerate(places):
        place = pl.ds(pl.multiple_of(offset, 16), piece.shape[0])
        copies.append(pltpu.make_async_copy(piece, whole.at[place, :], sems.at[first_sem + n]))
    for copy in copies:
        copy.start()
    return copies


def row_sum(values):
    return jnp.sum(values, axis=-1, keepdims=True)


def sam_kernel(counts, dims, sam_list, student, arrived, *rest):
    sam_pieces, dino_pieces = rest[: counts[0]], rest[counts[0] : sum(counts)]
    grad, predicted, dino_whole, rows_in, sam_whole, delta, rows_of, sems = rest[sum(counts) :]
    rows_copy = pltpu.make_async_copy(student, rows_in, sems.at[0])
    rows_copy.start()
    sam_copies = load_whole(sam_pieces, True, sam_whole, sems, 1)
    dino_copies = load_whole(dino_pieces, False, dino_whole, sems, 1 + counts[0])
    slots, per_device, image_dev, capacity = dims
    rank = lax.axis_index("img")
    arrived_rows(sam_list, rank, slots, per_device, image_dev, capacity, rows_of)
    for copy in (rows_copy, *sam_copies):
        copy.wait()
    sam_predicted = jnp.dot(rows_in[...], sam_whole[...], preferred_element_type=F32)
    patch = rows_in.shape[0] // image_dev
    for k in range(image_dev):
        row = rows_of[k]
        at = jnp.maximum(row, 0)
        rows = slice(k * patch, (k + 1) * patch)
        for n in range(sam_whole.shape[1] // 128):
            columns = slice(n * 128, (n + 1) * 128)
            target = arrived[at, n * patch : (n + 1) * patch, :].astype(F32)
            error = jnp.clip(sam_predicted[rows, columns] - target, -1.0, 1.0)
            delta[rows, columns] = jnp.where(row >= 0, error, 0.0).astype(BF16)
    grad[...] = lax.dot_general(
        delta[...], sam_whole[...], (((1,), (1,)), ((), ())), preferred_element_type=F32
    ).astype(BF16)
    for copy in dino_copies:
        copy.wait()
    predicted[...] = jnp.dot(rows_in[...], dino_whole[...], preferred_element_type=F32)


def dino_kernel(
    here, core_side, edge_side, matrix, predicted, sam_grad, whole, out, stacked, target, delta
):
    even = lax.rem(lax.axis_index("sp"), 2) == 0
    images, blocks = here.shape[0], here.shape[1] // 8
    core = core_side[...].astype(F32)
    edge = edge_side[...].astype(F32)
    above = jnp.where(even, edge, core)
    below = jnp.where(even, core, edge)
    for k, values in enumerate((above, here[...].astype(F32), below)):
        for n in range(blocks):
            part = values[:, 8 * n : 8 * n + 8, :].reshape(images * 8, 128)
            stacked[k * images * 8 : (k + 1) * images * 8, n * 128 : (n + 1) * 128] = part.astype(BF16)
    both = jnp.dot(matrix[...], stacked[...], preferred_element_type=F32)
    rows = predicted.shape[0]
    both = (both[: 2 * rows] + both[2 * rows :]).astype(BF16)
    for n in range(blocks):
        for side in range(2):
            at = (2 * n + side) * 128
            target[:, at : at + 128] = both[side * rows : (side + 1) * rows, n * 128 : (n + 1) * 128]
    p = predicted[...]
    t = target[...].astype(F32)
    pred_inv = 1.0 / jnp.sqrt(row_sum(p * p) + EPSILON)
    goal_inv = 1.0 / jnp.sqrt(row_sum(t * t) + EPSILON)
    cosine = row_sum(p * t) * pred_inv * goal_inv
    features = p.shape[-1]
    delta[...] = (
        (features * pred_inv) * ((cosine * pred_inv) * p - goal_inv * t)
    ).astype(BF16)
    back = lax.dot_general(
        delta[...], whole[...], (((1,), (1,)), ((), ())), preferred_element_type=F32
    )
    total = back.astype(BF16).astype(F32) + sam_grad[...].astype(F32)
    out[...] = total.astype(BF16)


def after(first, *rest):
    return lax.optimization_barrier((first, *rest))


def pair_perms(count):
    core = [(i, i ^ 1) for i in range(count)]
    edge = []
    for i in range(1, count - 1, 2):
        edge += [(i, i + 1), (i + 1, i)]
    return core, edge


def shards(
    student,
    dino_feats,
    sam_feats,
    dino_proj,
    sam_proj,
    dino_list,
    sam_list,
    dino_row_weight,
    dino_col_weight,
    sam_start,
    sam_row_weight,
    sam_col_weight,
):
    peers = lax.axis_size("img")
    sp_count = lax.axis_size("sp")
    images, rows_dev, patch_cols, width = student.shape
    slots = dino_list.shape[0]
    per_device = slots // peers
    capacity = (2 * per_device + peers - 1) // peers
    buffer_rows = peers * capacity
    patch = rows_dev * patch_cols
    grid_rows = dino_row_weight.shape[0]
    dino_cols, dino_width = dino_feats.shape[2:]
    sam_rows, sam_cols, sam_width = sam_feats.shape[1:]
    core_perm, edge_perm = pair_perms(sp_count)

    def core_swap(values):
        return lax.ppermute(values, "sp", core_perm)

    def edge_swap(values):
        return lax.ppermute(values, "sp", edge_perm)

    dims = (per_device, images, capacity)
    shared = sp_count == 4 and peers % 2 == 0
    pack_rows = patch * sam_width // 128 + dino_cols * dino_width // 128
    half_shape = jax.ShapeDtypeStruct((per_device, patch_cols, sam_width), BF16)
    own, core_part, edge_part = pl.pallas_call(
        functools.partial(pre_kernel, (per_device, grid_rows)),
        out_shape=(
            jax.ShapeDtypeStruct((per_device, patch, sam_width), F32),
            half_shape,
            half_shape,
        ),
        in_specs=[SMEM] * 2 + [VMEM] * 2,
        out_specs=(VMEM,) * 3,
        compiler_params=params(ALL_BYTES),
        name="pre",
    )(
        sam_start,
        sam_row_weight.T,
        sam_col_weight,
        sam_feats.reshape(per_device, sam_rows * sam_cols, sam_width),
    )
    edge_got = edge_swap(edge_part)
    core_got = core_swap(core_part)
    packed = pl.pallas_call(
        functools.partial(pack_kernel, dims),
        out_shape=jax.ShapeDtypeStruct((buffer_rows, pack_rows, 128), BF16),
        in_specs=[SMEM] * 2 + [VMEM] * 4,
        out_specs=VMEM,
        compiler_params=params(ALL_BYTES),
        name="pack",
    )(
        dino_list,
        sam_list,
        dino_feats.reshape(per_device, dino_cols, dino_width),
        own,
        core_got,
        edge_got,
    )

    arrived = lax.all_to_all(packed, "img", split_axis=0, concat_axis=0, tiled=True)

    rows = student.reshape(images * patch, width)
    matrix = pl.pallas_call(
        functools.partial(tables_kernel, images),
        out_shape=jax.ShapeDtypeStruct((4 * images * patch, 6 * images * dino_cols), BF16),
        in_specs=[SMEM, VMEM, ANY],
        out_specs=VMEM,
        compiler_params=params(),
        name="tables",
    )(dino_row_weight.T, dino_col_weight, rows)
    if shared:
        chip_perm = [(i, i ^ 2) for i in range(4)]
        near_perm = [(i, i ^ 1) for i in range(peers)]
        half = sam_proj.shape[0] // 2
        near = lax.dynamic_slice_in_dim(sam_proj, lax.axis_index("img") % 2 * half, half, 0)
        _, _, near = after(edge_got, core_got, near)
        sam_far = [lax.ppermute(near, "sp", chip_perm)]
        sam_far[0], _, dino_shard = after(sam_far[0], packed, dino_proj)
        sam_far.append(lax.ppermute(sam_far[0], "img", near_perm))
        dino_far = [
            lax.ppermute(part, "sp", chip_perm) for part in (dino_shard[:half], dino_shard[half:])
        ]
        matrix, dino_far[1] = after(matrix, dino_far[1])
        dino_pieces = [dino_proj, core_swap(dino_proj), *dino_far, *map(core_swap, dino_far)]
        sam_pieces = [sam_proj, core_swap(sam_proj), *sam_far, *map(core_swap, sam_far)]
    else:
        dino_pieces = [lax.all_gather(dino_proj, "sp", axis=0, tiled=True)]
        sam_pieces = [lax.all_gather(sam_proj, "sp", axis=0, tiled=True)]

    dino_rows = dino_cols * dino_width // 128
    chosen = pl.pallas_call(
        functools.partial(select_kernel, (slots, *dims)),
        out_shape=jax.ShapeDtypeStruct((images, dino_rows, 128), BF16),
        in_specs=[SMEM, VMEM],
        out_specs=VMEM,
        scratch_shapes=[pltpu.SMEM((images,), jnp.int32)],
        compiler_params=params(),
        name="select",
    )(dino_list, arrived)
    chosen_core, chosen_edge = core_swap(chosen), edge_swap(chosen)

    counts = (len(sam_pieces), len(dino_pieces))
    sam_grad, dino_predicted, dino_whole = pl.pallas_call(
        functools.partial(sam_kernel, counts, (slots, *dims)),
        out_shape=(
            jax.ShapeDtypeStruct(rows.shape, BF16),
            jax.ShapeDtypeStruct((rows.shape[0], dino_width), F32),
            jax.ShapeDtypeStruct((width, dino_width), BF16),
        ),
        in_specs=[SMEM, ANY, VMEM] + [ANY] * sum(counts),
        out_specs=(VMEM,) * 3,
        scratch_shapes=[
            pltpu.VMEM(rows.shape, BF16),
            pltpu.VMEM((width, sam_width), BF16),
            pltpu.VMEM((rows.shape[0], sam_width), BF16),
            pltpu.SMEM((images,), jnp.int32),
            pltpu.SemaphoreType.DMA((1 + sum(counts),)),
        ],
        compiler_params=params(),
        name="sam",
    )(sam_list, rows, arrived, *sam_pieces, *dino_pieces)
    out = pl.pallas_call(
        dino_kernel,
        out_shape=jax.ShapeDtypeStruct(rows.shape, BF16),
        in_specs=[VMEM] * 7,
        out_specs=VMEM,
        scratch_shapes=[
            pltpu.VMEM((6 * images * dino_cols, dino_width // 2), BF16),
            pltpu.VMEM((rows.shape[0], dino_width), BF16),
            pltpu.VMEM((rows.shape[0], dino_width), BF16),
        ],
        compiler_params=params(),
        name="dino",
    )(chosen, chosen_core, chosen_edge, matrix, dino_predicted, sam_grad, dino_whole)
    return out.reshape(student.shape)


def solution(mesh):
    placed = (
        P("img", "sp", None, None),
        P("img", "sp", None, None),
        P("img", "sp", None, None),
        P("sp", None),
        P("sp", None),
        P(),
        P(),
        P(),
        P(),
        P(),
        P(),
        P(),
    )
    return jax.shard_map(
        shards, mesh=mesh, in_specs=placed, out_specs=P("img", "sp", None, None), check_vma=False
    )
```

```python
import functools

import jax
import jax.numpy as jnp
from jax import lax
from jax.experimental import pallas as pl
from jax.experimental.pallas import tpu as pltpu
from jax.sharding import PartitionSpec as P

EPSILON = 1e-06
BF16 = jnp.bfloat16
F32 = jnp.float32
SMEM = pl.BlockSpec(memory_space=pltpu.SMEM)
VMEM = pl.BlockSpec(memory_space=pltpu.VMEM)
ANY = pl.BlockSpec(memory_space=pl.ANY)
VMEM_BYTES = 24 * 1024 * 1024
ALL_BYTES = 60 * 1024 * 1024


def params(vmem_bytes=VMEM_BYTES):
    return pltpu.CompilerParams(vmem_limit_bytes=vmem_bytes)


def split_dot(matrix, values):
    rows = matrix.shape[0]
    high = matrix.astype(BF16)
    low = (matrix - high.astype(F32)).astype(BF16)
    both = jnp.concatenate([high, low], axis=0)
    product = jnp.dot(both, values, preferred_element_type=F32)
    return product[:rows] + product[rows:]


def own_rows(list_ref, rank, per_device, image_dev, capacity):
    first = rank * per_device
    owners = [lax.div(list_ref[first + i], image_dev) for i in range(per_device)]
    rows = []
    for i in range(per_device):
        position = jnp.int32(0)
        for j in range(i):
            position = position + jnp.where(owners[j] == owners[i], 1, 0)
        rows.append(owners[i] * capacity + position)
    return rows


def arrived_rows(list_ref, rank, slots, per_device, image_dev, capacity, row_of):
    for k in range(image_dev):
        row_of[k] = -1

    def source(peer, _):
        def slot(i, seen):
            local = list_ref[peer * per_device + i] - rank * image_dev
            mine = jnp.logical_and(local >= 0, local < image_dev)

            @pl.when(mine)
            def _():
                row_of[local] = peer * capacity + seen

            return seen + jnp.where(mine, 1, 0)

        lax.fori_loop(0, per_device, slot, jnp.int32(0), unroll=True)
        return 0

    lax.fori_loop(0, slots // per_device, source, 0)


def pre_kernel(dims, start, row_weight, col_weight, sam_feats, own, core_part, edge_part):
    per_device, grid_rows = dims
    sp = lax.axis_index("sp")
    even = lax.rem(sp, 2) == 0
    up, down = 2 * sp - 1, 2 * sp + 2
    targets = [2 * sp, 2 * sp + 1, jnp.where(even, down, up), jnp.where(even, up, down)]
    col_count = col_weight.shape[1]
    across = jnp.concatenate([col_weight[...]] * 4, axis=1)
    column_row = lax.broadcasted_iota(jnp.int32, across.shape, 1) // col_count
    blocks = []
    for y in targets:
        inside = jnp.logical_and(y >= 0, y < grid_rows)
        line = jnp.clip(y, 0, grid_rows - 1)
        first_row = start[line] - 4 * sp
        taps = jnp.zeros(across.shape, F32)
        for tap in range(row_weight.shape[0]):
            weight = jnp.where(inside, row_weight[tap, line], 0.0)
            taps = taps + jnp.where(column_row == first_row + tap, weight, 0.0)
        blocks.append(across * taps)
    matrix = jnp.concatenate(blocks, axis=0)
    wide = own.shape[1]
    half = wide // 2
    for i in range(per_device):
        result = split_dot(matrix, sam_feats[i])
        own[i] = result[:wide]
        core_part[i] = result[wide : wide + half].astype(BF16)
        edge_part[i] = result[wide + half :].astype(BF16)


def pack_kernel(
    dims, dino_list, sam_list, dino_feats, own, core_part, edge_part, packed
):
    per_device, image_dev, capacity = dims
    rank = lax.axis_index("img")
    even = lax.rem(lax.axis_index("sp"), 2) == 0
    half, sam_width = core_part.shape[1:]
    patch = 2 * half
    sam_blocks = sam_width // 128
    for i, row in enumerate(own_rows(sam_list, rank, per_device, image_dev, capacity)):
        core = core_part[i].astype(F32)
        edge = edge_part[i].astype(F32)
        top = own[i, :half] + jnp.where(even, edge, core)
        bottom = own[i, half:] + jnp.where(even, core, edge)
        values = jnp.concatenate([top, bottom], axis=0).astype(BF16)
        for n in range(sam_blocks):
            packed[row, n * patch : (n + 1) * patch, :] = values[:, n * 128 : (n + 1) * 128]
    first = sam_blocks * patch
    packed[:, first:, :] = jnp.zeros((packed.shape[0], packed.shape[1] - first, 128), BF16)
    for i, row in enumerate(own_rows(dino_list, rank, per_device, image_dev, capacity)):
        values = dino_feats[i].astype(F32)
        blocks = [values[:, n * 128 : (n + 1) * 128] for n in range(values.shape[1] // 128)]
        packed[row, first:, :] = jnp.concatenate(blocks, axis=0).astype(BF16)


def tables_kernel(
    image_dev, row_weight, col_weight, student, matrix
):
    sp = lax.axis_index("sp")
    patch_cols, cols = col_weight.shape
    shape = (patch_cols, 3 * image_dev * 2 * cols)
    column = lax.broadcasted_iota(jnp.int32, shape, 1)
    tap_of = column // (image_dev * 2 * cols)
    image_of = (column // (2 * cols)) % image_dev
    block_of = (column // cols) % 2
    j_of = column % cols
    across = jnp.zeros(shape, F32)
    for j in range(cols):
        across = across + jnp.where(j_of == j, col_weight[:, j : j + 1], 0.0)
    lines = []
    for y in range(2):
        taps = jnp.zeros(shape, F32)
        for k in range(3):
            taps = taps + jnp.where(tap_of == k, row_weight[k, 2 * sp + y], 0.0)
        lines.append(across * taps)
    base = jnp.concatenate(lines, axis=0)
    image_of = jnp.concatenate([image_of] * 2, axis=0)
    block_of = jnp.concatenate([block_of] * 2, axis=0)
    high = base.astype(BF16).astype(F32)
    patch = base.shape[0]
    for part, values in enumerate((high, base - high)):
        for side in range(2):
            for k in range(image_dev):
                at = ((part * 2 + side) * image_dev + k) * patch
                mine = jnp.logical_and(image_of == k, block_of == side)
                matrix[at : at + patch, :] = jnp.where(mine, values, 0.0).astype(BF16)


def select_kernel(dims, dino_list, arrived, chosen, rows_of):
    slots, per_device, image_dev, capacity = dims
    rank = lax.axis_index("img")
    arrived_rows(dino_list, rank, slots, per_device, image_dev, capacity, rows_of)
    first = arrived.shape[1] - chosen.shape[1]
    for k in range(chosen.shape[0]):
        row = rows_of[k]
        values = arrived[jnp.maximum(row, 0), first:, :]
        chosen[k] = jnp.where(row >= 0, values, jnp.zeros_like(values))


def load_whole(pieces, by_neighbour, whole, sems, first_sem):
    rows = pieces[0].shape[0]
    places = [(pieces[0], 0)]
    if len(pieces) > 1:
        sp = lax.axis_index("sp")
        here, core = sp // 2 * 2, lax.rem(sp, 2)
        first = lax.rem(lax.axis_index("img"), 2) * (rows // 2) if by_neighbour else 0
        places = [(pieces[0], (here + core) * rows), (pieces[1], (here + 1 - core) * rows)]
        for far, at in ((2 - here + core, 2), (3 - here - core, 4)):
            places.append((pieces[at], far * rows + first))
            places.append((pieces[at + 1], far * rows + rows // 2 - first))
    copies = []
    for n, (piece, offset) in enumerate(places):
        place = pl.ds(pl.multiple_of(offset, 16), piece.shape[0])
        copies.append(pltpu.make_async_copy(piece, whole.at[place, :], sems.at[first_sem + n]))
    for copy in copies:
        copy.start()
    return copies


def row_sum(values):
    return jnp.sum(values, axis=-1, keepdims=True)


def sam_kernel(counts, dims, sam_list, student, arrived, *rest):
    sam_pieces, dino_pieces = rest[: counts[0]], rest[counts[0] : sum(counts)]
    grad, predicted, dino_whole, rows_in, sam_whole, delta, rows_of, sems = rest[sum(counts) :]
    rows_copy = pltpu.make_async_copy(student, rows_in, sems.at[0])
    rows_copy.start()
    sam_copies = load_whole(sam_pieces, True, sam_whole, sems, 1)
    dino_copies = load_whole(dino_pieces, False, dino_whole, sems, 1 + counts[0])
    slots, per_device, image_dev, capacity = dims
    rank = lax.axis_index("img")
    arrived_rows(sam_list, rank, slots, per_device, image_dev, capacity, rows_of)
    for copy in (rows_copy, *sam_copies):
        copy.wait()
    sam_predicted = jnp.dot(rows_in[...], sam_whole[...], preferred_element_type=F32)
    patch = rows_in.shape[0] // image_dev
    for k in range(image_dev):
        row = rows_of[k]
        at = jnp.maximum(row, 0)
        rows = slice(k * patch, (k + 1) * patch)
        for n in range(sam_whole.shape[1] // 128):
            columns = slice(n * 128, (n + 1) * 128)
            target = arrived[at, n * patch : (n + 1) * patch, :].astype(F32)
            error = jnp.clip(sam_predicted[rows, columns] - target, -1.0, 1.0)
            delta[rows, columns] = jnp.where(row >= 0, error, 0.0).astype(BF16)
    grad[...] = lax.dot_general(
        delta[...], sam_whole[...], (((1,), (1,)), ((), ())), preferred_element_type=F32
    ).astype(BF16)
    for copy in dino_copies:
        copy.wait()
    predicted[...] = jnp.dot(rows_in[...], dino_whole[...], preferred_element_type=F32)


def dino_kernel(
    here, core_side, edge_side, matrix, predicted, sam_grad, whole, out, stacked, target, delta
):
    even = lax.rem(lax.axis_index("sp"), 2) == 0
    images, blocks = here.shape[0], here.shape[1] // 8
    core = core_side[...].astype(F32)
    edge = edge_side[...].astype(F32)
    above = jnp.where(even, edge, core)
    below = jnp.where(even, core, edge)
    for k, values in enumerate((above, here[...].astype(F32), below)):
        for n in range(blocks):
            part = values[:, 8 * n : 8 * n + 8, :].reshape(images * 8, 128)
            stacked[k * images * 8 : (k + 1) * images * 8, n * 128 : (n + 1) * 128] = part.astype(BF16)
    both = jnp.dot(matrix[...], stacked[...], preferred_element_type=F32)
    rows = predicted.shape[0]
    both = (both[: 2 * rows] + both[2 * rows :]).astype(BF16)
    for n in range(blocks):
        for side in range(2):
            at = (2 * n + side) * 128
            target[:, at : at + 128] = both[side * rows : (side + 1) * rows, n * 128 : (n + 1) * 128]
    p = predicted[...]
    t = target[...].astype(F32)
    pred_inv = 1.0 / jnp.sqrt(row_sum(p * p) + EPSILON)
    goal_inv = 1.0 / jnp.sqrt(row_sum(t * t) + EPSILON)
    cosine = row_sum(p * t) * pred_inv * goal_inv
    features = p.shape[-1]
    delta[...] = (
        (features * pred_inv) * ((cosine * pred_inv) * p - goal_inv * t)
    ).astype(BF16)
    back = lax.dot_general(
        delta[...], whole[...], (((1,), (1,)), ((), ())), preferred_element_type=F32
    )
    total = back.astype(BF16).astype(F32) + sam_grad[...].astype(F32)
    out[...] = total.astype(BF16)


def after(first, *rest):
    return lax.optimization_barrier((first, *rest))


def pair_perms(count):
    core = [(i, i ^ 1) for i in range(count)]
    edge = []
    for i in range(1, count - 1, 2):
        edge += [(i, i + 1), (i + 1, i)]
    return core, edge


def shards(
    student,
    dino_feats,
    sam_feats,
    dino_proj,
    sam_proj,
    dino_list,
    sam_list,
    dino_row_weight,
    dino_col_weight,
    sam_start,
    sam_row_weight,
    sam_col_weight,
):
    peers = lax.axis_size("img")
    sp_count = lax.axis_size("sp")
    images, rows_dev, patch_cols, width = student.shape
    slots = dino_list.shape[0]
    per_device = slots // peers
    capacity = (2 * per_device + peers - 1) // peers
    buffer_rows = peers * capacity
    patch = rows_dev * patch_cols
    grid_rows = dino_row_weight.shape[0]
    dino_cols, dino_width = dino_feats.shape[2:]
    sam_rows, sam_cols, sam_width = sam_feats.shape[1:]
    core_perm, edge_perm = pair_perms(sp_count)

    def core_swap(values):
        return lax.ppermute(values, "sp", core_perm)

    def edge_swap(values):
        return lax.ppermute(values, "sp", edge_perm)

    dims = (per_device, images, capacity)
    shared = sp_count == 4 and peers % 2 == 0
    pack_rows = patch * sam_width // 128 + dino_cols * dino_width // 128
    half_shape = jax.ShapeDtypeStruct((per_device, patch_cols, sam_width), BF16)
    own, core_part, edge_part = pl.pallas_call(
        functools.partial(pre_kernel, (per_device, grid_rows)),
        out_shape=(
            jax.ShapeDtypeStruct((per_device, patch, sam_width), F32),
            half_shape,
            half_shape,
        ),
        in_specs=[SMEM] * 2 + [VMEM] * 2,
        out_specs=(VMEM,) * 3,
        compiler_params=params(ALL_BYTES),
        name="pre",
    )(
        sam_start,
        sam_row_weight.T,
        sam_col_weight,
        sam_feats.reshape(per_device, sam_rows * sam_cols, sam_width),
    )
    edge_got = edge_swap(edge_part)
    core_got = core_swap(core_part)
    packed = pl.pallas_call(
        functools.partial(pack_kernel, dims),
        out_shape=jax.ShapeDtypeStruct((buffer_rows, pack_rows, 128), BF16),
        in_specs=[SMEM] * 2 + [VMEM] * 4,
        out_specs=VMEM,
        compiler_params=params(ALL_BYTES),
        name="pack",
    )(
        dino_list,
        sam_list,
        dino_feats.reshape(per_device, dino_cols, dino_width),
        own,
        core_got,
        edge_got,
    )

    arrived = lax.all_to_all(packed, "img", split_axis=0, concat_axis=0, tiled=True)

    rows = student.reshape(images * patch, width)
    matrix = pl.pallas_call(
        functools.partial(tables_kernel, images),
        out_shape=jax.ShapeDtypeStruct((4 * images * patch, 6 * images * dino_cols), BF16),
        in_specs=[SMEM, VMEM, ANY],
        out_specs=VMEM,
        compiler_params=params(),
        name="tables",
    )(dino_row_weight.T, dino_col_weight, rows)
    if shared:
        chip_perm = [(i, i ^ 2) for i in range(4)]
        near_perm = [(i, i ^ 1) for i in range(peers)]
        half = sam_proj.shape[0] // 2
        near = lax.dynamic_slice_in_dim(sam_proj, lax.axis_index("img") % 2 * half, half, 0)
        _, _, near = after(edge_got, core_got, near)
        sam_far = [lax.ppermute(near, "sp", chip_perm)]
        sam_far[0], _, dino_shard = after(sam_far[0], packed, dino_proj)
        sam_far.append(lax.ppermute(sam_far[0], "img", near_perm))
        dino_far = [
            lax.ppermute(part, "sp", chip_perm) for part in (dino_shard[:half], dino_shard[half:])
        ]
        matrix, dino_far[1] = after(matrix, dino_far[1])
        dino_pieces = [dino_proj, core_swap(dino_proj), *dino_far, *map(core_swap, dino_far)]
        sam_pieces = [sam_proj, core_swap(sam_proj), *sam_far, *map(core_swap, sam_far)]
    else:
        dino_pieces = [lax.all_gather(dino_proj, "sp", axis=0, tiled=True)]
        sam_pieces = [lax.all_gather(sam_proj, "sp", axis=0, tiled=True)]

    dino_rows = dino_cols * dino_width // 128
    chosen = pl.pallas_call(
        functools.partial(select_kernel, (slots, *dims)),
        out_shape=jax.ShapeDtypeStruct((images, dino_rows, 128), BF16),
        in_specs=[SMEM, VMEM],
        out_specs=VMEM,
        scratch_shapes=[pltpu.SMEM((images,), jnp.int32)],
        compiler_params=params(),
        name="select",
    )(dino_list, arrived)
    chosen_core, chosen_edge = core_swap(chosen), edge_swap(chosen)

    counts = (len(sam_pieces), len(dino_pieces))
    sam_grad, dino_predicted, dino_whole = pl.pallas_call(
        functools.partial(sam_kernel, counts, (slots, *dims)),
        out_shape=(
            jax.ShapeDtypeStruct(rows.shape, BF16),
            jax.ShapeDtypeStruct((rows.shape[0], dino_width), F32),
            jax.ShapeDtypeStruct((width, dino_width), BF16),
        ),
        in_specs=[SMEM, ANY, VMEM] + [ANY] * sum(counts),
        out_specs=(VMEM,) * 3,
        scratch_shapes=[
            pltpu.VMEM(rows.shape, BF16),
            pltpu.VMEM((width, sam_width), BF16),
            pltpu.VMEM((rows.shape[0], sam_width), BF16),
            pltpu.SMEM((images,), jnp.int32),
            pltpu.SemaphoreType.DMA((1 + sum(counts),)),
        ],
        compiler_params=params(),
        name="sam",
    )(sam_list, rows, arrived, *sam_pieces, *dino_pieces)
    out = pl.pallas_call(
        dino_kernel,
        out_shape=jax.ShapeDtypeStruct(rows.shape, BF16),
        in_specs=[VMEM] * 7,
        out_specs=VMEM,
        scratch_shapes=[
            pltpu.VMEM((6 * images * dino_cols, dino_width // 2), BF16),
            pltpu.VMEM((rows.shape[0], dino_width), BF16),
            pltpu.VMEM((rows.shape[0], dino_width), BF16),
        ],
        compiler_params=params(),
        name="dino",
    )(chosen, chosen_core, chosen_edge, matrix, dino_predicted, sam_grad, dino_whole)
    return out.reshape(student.shape)


def solution(mesh):
    placed = (
        P("img", "sp", None, None),
        P("img", "sp", None, None),
        P("img", "sp", None, None),
        P("sp", None),
        P("sp", None),
        P(),
        P(),
        P(),
        P(),
        P(),
        P(),
        P(),
    )
    return jax.shard_map(
        shards, mesh=mesh, in_specs=placed, out_specs=P("img", "sp", None, None), check_vma=False
    )
```
